32 devices in a mesh: groups: 2 (over x), wide: 16 (over z, y, core).
Axes of the slice: x: 2, y: 2, z: 4, core: 2. Of those that a mesh axis runs over, the one named last changes fastest.
Arguments:
- tokens: bfloat16 [512, 16384], P(('groups', 'wide')), parts along dimension 0, may hold values from -6 to 6
- base_weight: bfloat16 [16384, 16384], P(None, 'wide'), may hold values from -0.046875 to 0.046875
- shrink_blocks: bfloat16 [128, 16, 16384], P('wide'), may hold values from -0.046875 to 0.046875
- expand_blocks: bfloat16 [128, 16, 16384], P('wide'), may hold values from -1.5 to 1.5
- adapter_slot: int32 [128], replicated, may hold values from 0 to 127, each once
- seg_adapter: int32 [32, 4], P(('groups', 'wide')), parts along dimension 0, may hold values from 0 to 127
- seg_lengths: int32 [32, 4], P(('groups', 'wide')), parts along dimension 0, may hold values from 1 to 4, 12 in all within a row
Outputs:
- queries: bfloat16 [512, 16384], P(('groups', 'wide')), parts along dimension 0
The draws below stay inside these ranges and needn't reach their ends.
There are 2 independent parts, one for each index of `groups`. The reference program is written for one: setup_inputs(seed, part) draws one part's arguments, and reference() takes and returns one part's arrays. A program takes and returns all parts, laid end to end along the dimension named above; an argument that names none is the same for every part. Nothing has to cross between parts.
Inputs may be any that keep to these rules, and one draw needn't show every extreme that they name: Adapter i's blocks stand at index adapter_slot[i] of shrink_blocks and expand_blocks; each slot is used once. `seg_lengths`: the 4 lengths of one index of wide sum to 12.
All inputs are finite; a program needn't handle non-finite values.
Results may differ from the reference program's by a relative error of at most 0.0048.
Values may be sent and summed in bfloat16 or wider, within the bound.
A program may use at most 128 MiB of HBM per device.

```python
import math
import jax
import jax.numpy as jnp
import numpy as np
from jax import lax

D = 16384
R = 16
SEG_CAP = 4
SEG_DEV = 4
TOKENS = 256
ADAPTERS = 128
N_WIDE = 16


def touch_ends(array, key, low, top_value):
    longest = array.shape.index(max(array.shape))
    spots = []
    for shift in (0, 1):
        where = [jax.random.randint(jax.random.fold_in(key, axis), (), 0, length) for axis, length in enumerate(array.shape)]
        where[longest] = (where[longest] + shift) % array.shape[longest]
        spots.append(tuple(where))
    return array.at[spots[0]].set(low).at[spots[1]].set(top_value)


def levels(key, dims, split, least, top_value):
    gain = 1.0
    for axis_at, parts in split:
        heights = jax.random.uniform(jax.random.fold_in(jax.random.fold_in(key, 6), axis_at), (parts,), jnp.float32, least / len(split), top_value / len(split))
        gain = gain * jnp.repeat(jnp.exp(heights), dims[axis_at] // parts).reshape((-1,) + (1,) * (len(dims) - 1 - axis_at))
    return gain


def rank_table(count, lean):
    loads = [(1 << 20) // math.isqrt(standing ** lean) + 1 for standing in range(1, count + 1)]
    scale = 1 + sum(loads) // (1 << 30)
    return np.cumsum(np.array([max(1, weight // scale) for weight in loads]))


def ranked_ids(key, shape, amount, slope):
    table = rank_table(amount, slope)
    ticket = jax.random.randint(jax.random.fold_in(key, 1), shape, 0, int(table[amount - 1]))
    grade = jnp.searchsorted(jnp.asarray(table, jnp.int32), ticket, side="right")
    return jax.random.permutation(jax.random.fold_in(key, 2), amount)[grade].astype(jnp.int32)


def length_profile(count, total, bound, slope):
    portions = [(1 << 20) // math.isqrt(grade ** slope) + 1 for grade in range(2, count + 1)]
    rest, holding = total - bound - (count - 1), [1] * (count - 1)
    while rest > 0:
        candidates = [i for i in range(count - 1) if holding[i] < bound]
        whole, left = sum([portions[i] for i in candidates]), rest
        for i in candidates:
            more = min(bound - holding[i], max(1, left * portions[i] // whole), rest)
            holding[i] = holding[i] + more
            rest = rest - more
    return np.array([bound] + holding)


def ragged_sizes(key, amount, total, bound, skew):
    if amount == 2:
        one = jax.random.randint(key, (), max(1, total - bound), min(bound, total - 1) + 1)
        return jnp.stack([one, total - one])
    lengths = jnp.asarray(length_profile(amount, total, bound, skew), jnp.int32)
    couples = (amount - 1) // 2
    giver, sink = lengths[1:1 + 2 * couples:2], lengths[2:2 + 2 * couples:2]
    slack = jnp.minimum(giver - 1, bound - sink)
    moved = jax.random.randint(jax.random.fold_in(key, 1), (couples,), 0, 1 << 20) % (slack + 1)
    lengths = lengths.at[1:1 + 2 * couples:2].set(giver - moved).at[2:2 + 2 * couples:2].set(sink + moved)
    return lengths[jax.random.permutation(jax.random.fold_in(key, 2), amount)]


def centred(key, extent, scale, most, cuts=(), kind=jnp.bfloat16):
    entries = scale * jax.random.normal(key, extent, jnp.float32)
    if cuts:
        entries = entries * levels(key, extent, cuts, -0.22, 0.18)
    return jnp.clip(entries, -most, most).astype(kind)


def setup_inputs(seed: int = 0, part: int = 0) -> dict:
    splits = jax.random.split(jax.random.key(seed), 8)
    own_keys = jax.random.split(jax.random.fold_in(splits[7], part), 8)
    return {
        "tokens": centred(own_keys[0], (TOKENS, D), 1.0, 6.0, ((0, 16),)),
        "base_weight": centred(splits[1], (D, D), D ** -0.5, 0.046875, ((1, 16),)),
        "shrink_blocks": centred(splits[2], (ADAPTERS, R, D), D ** -0.5, 0.046875, ((0, 16),)),
        "expand_blocks": centred(splits[3], (ADAPTERS, R, D), R ** -0.5, 1.5, ((0, 16),)),
        "adapter_slot": jax.random.permutation(splits[4], ADAPTERS).astype(jnp.int32),
        "seg_adapter": touch_ends(ranked_ids(own_keys[5], (N_WIDE, SEG_DEV), ADAPTERS, 2), jax.random.fold_in(own_keys[5], 3), 0, ADAPTERS - 1).astype(jnp.int32),
        "seg_lengths": jax.vmap(lambda own: ragged_sizes(own, SEG_DEV, 3 * SEG_DEV, SEG_CAP, 1))(jax.random.split(own_keys[6], N_WIDE)).reshape((N_WIDE, SEG_DEV)).astype(jnp.int32),
    }


def reference(tokens, base_weight, shrink_blocks, expand_blocks, adapter_slot, seg_adapter, seg_lengths):
    base_share = jnp.dot(tokens, base_weight, preferred_element_type=jnp.float32)
    shrink_flat = shrink_blocks.reshape(ADAPTERS * R, D)
    expand_weight_flattened = expand_blocks.reshape(ADAPTERS * R, D)
    shrink_full = lax.dot_general(tokens, shrink_flat, (((1,), (1,)), ((), ())), preferred_element_type=jnp.float32)
    row_adapter = jnp.repeat(seg_adapter.reshape(-1), SEG_CAP)
    row_length = jnp.repeat(seg_lengths.reshape(-1), SEG_CAP)
    position = jnp.arange(row_adapter.shape[0], dtype=jnp.int32) % SEG_CAP
    filled = position < row_length
    row_slot = jnp.take(adapter_slot, row_adapter)
    column_slot = jnp.arange(ADAPTERS * R, dtype=jnp.int32) // R
    selected = filled[:, None] & (row_slot[:, None] == column_slot[None, :])
    shrink_weight = jnp.where(selected, shrink_full, jnp.float32(0.0)).astype(jnp.bfloat16)
    adapter_update = jnp.dot(shrink_weight, expand_weight_flattened, preferred_element_type=jnp.float32).astype(jnp.bfloat16)
    return (base_share + adapter_update.astype(jnp.float32)).astype(jnp.bfloat16)
```

```python
import jax
import jax.numpy as jnp
from jax import lax
from jax.sharding import PartitionSpec as P


def body(tokens, base_weight, shrink_blocks, expand_blocks, adapter_slot, seg_adapter, seg_lengths):
    my_rows = tokens.shape[0]
    segment_cap = my_rows // seg_adapter.shape[1]
    local_count, rank_size, width = shrink_blocks.shape
    here = lax.axis_index("wide")
    peers = lax.axis_size("wide")
    position = jnp.arange(segment_cap, dtype=jnp.int32)
    my_slot = jnp.take(adapter_slot, seg_adapter.reshape(-1))
    my_row_slot = jnp.where(
        position[None, :] < seg_lengths.reshape(-1, 1), my_slot[:, None], -1
    ).reshape(1, my_rows)
    row_slot = lax.all_gather(my_row_slot, "wide", axis=0, tiled=True).reshape(-1)
    rows = lax.all_gather(tokens, "wide", axis=0, tiled=True)

    column_slot = (
        here * local_count + jnp.arange(local_count * rank_size, dtype=jnp.int32) // rank_size
    )
    selected = row_slot[:, None] == column_slot[None, :]
    shrink = lax.dot_general(
        rows,
        shrink_blocks.reshape(local_count * rank_size, width),
        (((1,), (1,)), ((), ())),
        preferred_element_type=jnp.float32,
    )
    shrink = jnp.where(selected, shrink, jnp.float32(0.0)).astype(jnp.bfloat16)
    delta = jnp.dot(
        shrink,
        expand_blocks.reshape(local_count * rank_size, width),
        preferred_element_type=jnp.float32,
    ).astype(jnp.bfloat16)
    update = lax.psum_scatter(delta, "wide", scatter_dimension=0, tiled=True)

    base = jnp.dot(rows, base_weight, preferred_element_type=jnp.float32).astype(jnp.bfloat16)
    base_rows = lax.all_to_all(
        base.reshape(peers, my_rows, -1), "wide", split_axis=0, concat_axis=0, tiled=True
    )
    base_rows = jnp.swapaxes(base_rows, 0, 1).reshape(my_rows, width)
    return (base_rows.astype(jnp.float32) + update.astype(jnp.float32)).astype(jnp.bfloat16)


def solution(mesh):
    placed = (
        P(("groups", "wide"), None),
        P(None, "wide"),
        P("wide", None, None),
        P("wide", None, None),
        P(),
        P(("groups", "wide"), None),
        P(("groups", "wide"), None),
    )
    return jax.shard_map(
        body, mesh=mesh, in_specs=placed, out_specs=P(("groups", "wide"), None), check_vma=False
    )
```

```python
import functools

import jax
import jax.numpy as jnp
from jax import lax
from jax.experimental import pallas as pl
from jax.experimental.pallas import tpu as pltpu
from jax.sharding import PartitionSpec as P


CHUNKS = 4
MESH = pl.DeviceIdType.MESH


def ring(n, snake):
    me = lax.axis_index("wide")
    chips = n // 2
    core, chip = me % 2, me // 2
    half = chips // 2

    def device(position, on_core):
        at = (position + chips) % chips
        if snake:
            back = at // half
            at = (1 - back) * (2 * at) + back * (2 * (chips - 1 - at) + 1)
        return at * 2 + on_core

    position = chip
    if snake:
        low, high = chip % 2, chip // 2
        position = (1 - low) * high + low * (chips - 1 - high)
    return me, core, position, device


def greet_all(n, me):
    barrier = pltpu.get_barrier_semaphore()
    for step in range(1, n):
        pl.semaphore_signal(
            barrier, inc=1, device_id={"wide": (me + step) % n}, device_id_type=MESH
        )
    pl.semaphore_wait(barrier, n - 1)


def gather_kernel(
    n, snake, tok, meta, out, meta_out, own_sem, meta_send, meta_recv,
    right_send, right_recv, left_send, left_recv, sib_send, sib_recv,
):
    me, core, position, device = ring(n, snake)
    chips = n // 2
    rows, width = tok.shape
    part = width // CHUNKS
    right_hops = chips // 2
    left_hops = chips - 1 - right_hops
    right, left, sibling = device(position + 1, core), device(position - 1, core), device(position, 1 - core)
    greet_all(n, me)

    def place(owner, k):
        return out.at[pl.ds(pl.multiple_of(owner * rows, rows), rows), pl.ds(k * part, part)]

    def copy(src, dst, send, recv, target):
        return pltpu.make_async_remote_copy(
            src_ref=src, dst_ref=dst, send_sem=send, recv_sem=recv,
            device_id={"wide": target}, device_id_type=MESH,
        )

    started = []
    for k in range(CHUNKS):
        src = tok.at[:, pl.ds(k * part, part)]
        started.append(copy(src, place(me, k), right_send.at[0, k], right_recv.at[0, k], right))
        started[-1].start()
        started.append(copy(src, place(me, k), left_send.at[0, k], left_recv.at[0, k], left))
        started[-1].start()
    for step in range(1, n):
        started.append(
            copy(meta, meta_out.at[me], meta_send.at[step], meta_recv.at[step], (me + step) % n)
        )
        started[-1].start()
    for k in range(CHUNKS):
        src = tok.at[:, pl.ds(k * part, part)]
        started.append(copy(src, place(me, k), sib_send.at[0, k], sib_recv.at[0, k], sibling))
        started[-1].start()
    own_rows = pltpu.make_async_copy(tok, out.at[pl.ds(pl.multiple_of(me * rows, rows), rows), :], own_sem.at[0])
    own_meta = pltpu.make_async_copy(meta, meta_out.at[me], own_sem.at[1])
    own_rows.start()
    own_meta.start()

    for hop in range(1, right_hops + 1):
        for k in range(CHUNKS):
            block = place(device(position - hop, core), k)
            copy(block, block, right_send.at[hop - 1, k], right_recv.at[hop - 1, k], right).wait_recv()
            if hop < right_hops:
                started.append(copy(block, block, right_send.at[hop, k], right_recv.at[hop, k], right))
                started[-1].start()
            started.append(copy(block, block, sib_send.at[hop, k], sib_recv.at[hop, k], sibling))
            started[-1].start()
            if hop <= left_hops:
                block = place(device(position + hop, core), k)
                copy(block, block, left_send.at[hop - 1, k], left_recv.at[hop - 1, k], left).wait_recv()
                if hop < left_hops:
                    started.append(copy(block, block, left_send.at[hop, k], left_recv.at[hop, k], left))
                    started[-1].start()
                at = right_hops + hop
                started.append(copy(block, block, sib_send.at[at, k], sib_recv.at[at, k], sibling))
                started[-1].start()

    for at in range(chips):
        source = position - at if at <= right_hops else position + at - right_hops
        for k in range(CHUNKS):
            block = place(device(source, 1 - core), k)
            copy(block, block, sib_send.at[at, k], sib_recv.at[at, k], sibling).wait_recv()
    for step in range(1, n):
        dst = meta_out.at[(me - step + n) % n]
        copy(meta, dst, meta_send.at[step], meta_recv.at[step], (me + step) % n).wait_recv()
    for one in started:
        one.wait_send()
    own_rows.wait()
    own_meta.wait()


def gather(tokens, meta, n, snake):
    rows, width = tokens.shape
    chips = n // 2
    hops = chips // 2
    dma = pltpu.SemaphoreType.DMA
    return pl.pallas_call(
        functools.partial(gather_kernel, n, snake),
        out_shape=(
            jax.ShapeDtypeStruct((n * rows, width), tokens.dtype),
            jax.ShapeDtypeStruct((n,) + meta.shape, meta.dtype),
        ),
        in_specs=[pl.BlockSpec(memory_space=pl.ANY)] * 2,
        out_specs=(pl.BlockSpec(memory_space=pl.ANY),) * 2,
        scratch_shapes=[
            dma((2,)), dma((n,)), dma((n,)),
            dma((hops, CHUNKS)), dma((hops, CHUNKS)), dma((hops, CHUNKS)), dma((hops, CHUNKS)),
            dma((chips, CHUNKS)), dma((chips, CHUNKS)),
        ],
        compiler_params=pltpu.CompilerParams(collective_id=0, has_side_effects=True),
    )(tokens, meta)


def body(snake, tokens, base_weight, shrink_blocks, expand_blocks, adapter_slot, seg_adapter, seg_lengths):
    my_rows = tokens.shape[0]
    segment_cap = my_rows // seg_adapter.shape[1]
    local_count, rank_size, width = shrink_blocks.shape
    here = lax.axis_index("wide")
    peers = lax.axis_size("wide")
    position = jnp.arange(segment_cap, dtype=jnp.int32)
    my_slot = jnp.take(adapter_slot, seg_adapter.reshape(-1))
    my_row_slot = jnp.where(
        position[None, :] < seg_lengths.reshape(-1, 1), my_slot[:, None], -1
    ).reshape(1, my_rows)
    meta = jnp.broadcast_to(jnp.pad(my_row_slot, ((0, 0), (0, 128 - my_rows))), (8, 128))
    rows, meta_all = gather(tokens, meta, peers, snake)
    row_slot = meta_all[:, 0, :my_rows].reshape(-1)

    column_slot = (
        here * local_count + jnp.arange(local_count * rank_size, dtype=jnp.int32) // rank_size
    )
    selected = row_slot[:, None] == column_slot[None, :]
    shrink = lax.dot_general(
        rows,
        shrink_blocks.reshape(local_count * rank_size, width),
        (((1,), (1,)), ((), ())),
        preferred_element_type=jnp.float32,
    )
    shrink = jnp.where(selected, shrink, jnp.float32(0.0)).astype(jnp.bfloat16)
    delta = jnp.dot(
        shrink,
        expand_blocks.reshape(local_count * rank_size, width),
        preferred_element_type=jnp.float32,
    ).astype(jnp.bfloat16)
    update = lax.psum_scatter(delta, "wide", scatter_dimension=0, tiled=True)

    base = jnp.dot(rows, base_weight, preferred_element_type=jnp.float32).astype(jnp.bfloat16)
    base_rows = lax.all_to_all(
        base.reshape(peers, my_rows, -1), "wide", split_axis=0, concat_axis=0, tiled=True
    )
    base_rows = jnp.swapaxes(base_rows, 0, 1).reshape(my_rows, width)
    return (base_rows.astype(jnp.float32) + update.astype(jnp.float32)).astype(jnp.bfloat16)


def solution(mesh):
    placed = (
        P(("groups", "wide"), None),
        P(None, "wide"),
        P("wide", None, None),
        P("wide", None, None),
        P(),
        P(("groups", "wide"), None),
        P(("groups", "wide"), None),
    )
    snake = mesh.shape["groups"] == 2
    return jax.shard_map(
        functools.partial(body, snake), mesh=mesh, in_specs=placed, out_specs=P(("groups", "wide"), None), check_vma=False
    )
```

```python
import functools

import jax
import jax.numpy as jnp
from jax import lax
from jax.experimental import pallas as pl
from jax.experimental.pallas import tpu as pltpu
from jax.sharding import PartitionSpec as P


CHUNKS = 4
MESH = pl.DeviceIdType.MESH


def ring(n, snake):
    me = lax.axis_index("wide")
    chips = n // 2
    core, chip = me % 2, me // 2
    half = chips // 2

    def device(position, on_core):
        at = (position + chips) % chips
        if snake:
            back = at // half
            at = (1 - back) * (2 * at) + back * (2 * (chips - 1 - at) + 1)
        return at * 2 + on_core

    position = chip
    if snake:
        low, high = chip % 2, chip // 2
        position = (1 - low) * high + low * (chips - 1 - high)
    return me, core, position, device


def greet_all(n, me):
    barrier = pltpu.get_barrier_semaphore()
    for step in range(1, n):
        pl.semaphore_signal(
            barrier, inc=1, device_id={"wide": (me + step) % n}, device_id_type=MESH
        )
    pl.semaphore_wait(barrier, n - 1)


def gather_kernel(
    n, snake, tok, meta, out, meta_out, own_sem, meta_send, meta_recv,
    right_send, right_recv, left_send, left_recv, sib_send, sib_recv,
):
    me, core, position, device = ring(n, snake)
    chips = n // 2
    rows, width = tok.shape
    part = width // CHUNKS
    right_hops = chips // 2
    left_hops = chips - 1 - right_hops
    right, left, sibling = device(position + 1, core), device(position - 1, core), device(position, 1 - core)
    greet_all(n, me)

    def place(owner, k):
        return out.at[pl.ds(pl.multiple_of(owner * rows, rows), rows), pl.ds(k * part, part)]

    def copy(src, dst, send, recv, target):
        return pltpu.make_async_remote_copy(
            src_ref=src, dst_ref=dst, send_sem=send, recv_sem=recv,
            device_id={"wide": target}, device_id_type=MESH,
        )

    started = []
    for k in range(CHUNKS):
        src = tok.at[:, pl.ds(k * part, part)]
        started.append(copy(src, place(me, k), right_send.at[0, k], right_recv.at[0, k], right))
        started[-1].start()
        started.append(copy(src, place(me, k), left_send.at[0, k], left_recv.at[0, k], left))
        started[-1].start()
    for step in range(1, n):
        started.append(
            copy(meta, meta_out.at[me], meta_send.at[step], meta_recv.at[step], (me + step) % n)
        )
        started[-1].start()
    for k in range(CHUNKS):
        src = tok.at[:, pl.ds(k * part, part)]
        started.append(copy(src, place(me, k), sib_send.at[0, k], sib_recv.at[0, k], sibling))
        started[-1].start()
    own_rows = pltpu.make_async_copy(tok, out.at[pl.ds(pl.multiple_of(me * rows, rows), rows), :], own_sem.at[0])
    own_meta = pltpu.make_async_copy(meta, meta_out.at[me], own_sem.at[1])
    own_rows.start()
    own_meta.start()

    for hop in range(1, right_hops + 1):
        for k in range(CHUNKS):
            block = place(device(position - hop, core), k)
            copy(block, block, right_send.at[hop - 1, k], right_recv.at[hop - 1, k], right).wait_recv()
            if hop < right_hops:
                started.append(copy(block, block, right_send.at[hop, k], right_recv.at[hop, k], right))
                started[-1].start()
            started.append(copy(block, block, sib_send.at[hop, k], sib_recv.at[hop, k], sibling))
            started[-1].start()
            if hop <= left_hops:
                block = place(device(position + hop, core), k)
                copy(block, block, left_send.at[hop - 1, k], left_recv.at[hop - 1, k], left).wait_recv()
                if hop < left_hops:
                    started.append(copy(block, block, left_send.at[hop, k], left_recv.at[hop, k], left))
                    started[-1].start()
                at = right_hops + hop
                started.append(copy(block, block, sib_send.at[at, k], sib_recv.at[at, k], sibling))
                started[-1].start()

    for at in range(chips):
        source = position - at if at <= right_hops else position + at - right_hops
        for k in range(CHUNKS):
            block = place(device(source, 1 - core), k)
            copy(block, block, sib_send.at[at, k], sib_recv.at[at, k], sibling).wait_recv()
    for step in range(1, n):
        dst = meta_out.at[(me - step + n) % n]
        copy(meta, dst, meta_send.at[step], meta_recv.at[step], (me + step) % n).wait_recv()
    for one in started:
        one.wait_send()
    own_rows.wait()
    own_meta.wait()


def gather(tokens, meta, n, snake):
    rows, width = tokens.shape
    chips = n // 2
    hops = chips // 2
    dma = pltpu.SemaphoreType.DMA
    return pl.pallas_call(
        functools.partial(gather_kernel, n, snake),
        out_shape=(
            jax.ShapeDtypeStruct((n * rows, width), tokens.dtype),
            jax.ShapeDtypeStruct((n,) + meta.shape, meta.dtype),
        ),
        in_specs=[pl.BlockSpec(memory_space=pl.ANY)] * 2,
        out_specs=(pl.BlockSpec(memory_space=pl.ANY),) * 2,
        scratch_shapes=[
            dma((2,)), dma((n,)), dma((n,)),
            dma((hops, CHUNKS)), dma((hops, CHUNKS)), dma((hops, CHUNKS)), dma((hops, CHUNKS)),
            dma((chips, CHUNKS)), dma((chips, CHUNKS)),
        ],
        compiler_params=pltpu.CompilerParams(collective_id=0, has_side_effects=True),
    )(tokens, meta)


def reduce_kernel(
    n, snake, delta, base, out, sib, from_left, from_right, pieces, base_send, base_recv,
    right_send, right_recv, left_send, left_recv, sib_send, sib_recv,
):
    me, core, position, device = ring(n, snake)
    chips = n // 2
    rows, width = out.shape
    part, piece = width // CHUNKS, width // n
    right_hops = chips // 2
    left_hops = chips - 1 - right_hops
    right, left, sibling = device(position + 1, core), device(position - 1, core), device(position, 1 - core)
    offsets = []
    for hop in range(right_hops):
        offsets.append(right_hops - hop)
        if hop < left_hops:
            offsets.append(hop - left_hops)
    offsets.append(0)
    greet_all(n, me)

    def block(owner):
        return pl.ds(pl.multiple_of(owner * rows, rows), rows)

    def columns(k):
        return pl.ds(k * part, part)

    def copy(src, dst, send, recv, target):
        return pltpu.make_async_remote_copy(
            src_ref=src, dst_ref=dst, send_sem=send, recv_sem=recv,
            device_id={"wide": target}, device_id_type=MESH,
        )

    def sib_copy(j, k):
        return copy(
            delta.at[block(device(position + offsets[j], 1 - core)), columns(k)],
            sib.at[j, :, columns(k)], sib_send.at[j, k], sib_recv.at[j, k], sibling,
        )

    def chip_sum(offset, k):
        j = offsets.index(offset)
        sib_copy(j, k).wait_recv()
        return sib[j, :, columns(k)] + delta[block(device(position + offset, core)), columns(k)]

    def base_copy(step):
        peer = (me + step) % n
        return copy(base.at[block(peer), :], pieces.at[me], base_send.at[step], base_recv.at[step], peer)

    started = []

    def start(one):
        one.start()
        started.append(one)

    def to_right(src, slot, k):
        start(copy(src, from_left.at[slot, :, columns(k)], right_send.at[slot, k], right_recv.at[slot, k], right))

    def to_left(src, slot, k):
        start(copy(src, from_right.at[slot, :, columns(k)], left_send.at[slot, k], left_recv.at[slot, k], left))

    for j in range(chips):
        for k in range(CHUNKS):
            start(sib_copy(j, k))
    for k in range(CHUNKS):
        j = offsets.index(right_hops)
        sib[j, :, columns(k)] = chip_sum(right_hops, k)
        to_right(sib.at[j, :, columns(k)], 0, k)
    for k in range(CHUNKS):
        j = offsets.index(-left_hops)
        sib[j, :, columns(k)] = chip_sum(-left_hops, k)
        to_left(sib.at[j, :, columns(k)], 0, k)
    for step in range(1, n):
        start(base_copy(step))
    pieces[me] = base[block(me), :]

    def right_arrival(slot, k):
        here = from_left.at[slot, :, columns(k)]
        copy(here, here, right_send.at[slot, k], right_recv.at[slot, k], right).wait_recv()

    def left_arrival(slot, k):
        here = from_right.at[slot, :, columns(k)]
        copy(here, here, left_send.at[slot, k], left_recv.at[slot, k], left).wait_recv()

    for hop in range(1, right_hops):
        for k in range(CHUNKS):
            own = chip_sum(right_hops - hop, k)
            right_arrival(hop - 1, k)
            from_left[hop - 1, :, columns(k)] = from_left[hop - 1, :, columns(k)] + own
            to_right(from_left.at[hop - 1, :, columns(k)], hop, k)
            if hop < left_hops:
                own = chip_sum(hop - left_hops, k)
                left_arrival(hop - 1, k)
                from_right[hop - 1, :, columns(k)] = from_right[hop - 1, :, columns(k)] + own
                to_left(from_right.at[hop - 1, :, columns(k)], hop, k)

    for step in range(1, n):
        sender = (me - step + n) % n
        copy(
            base.at[block(sender), :], pieces.at[sender], base_send.at[step], base_recv.at[step], sender
        ).wait_recv()
    for k in range(CHUNKS):
        own = chip_sum(0, k)
        left_arrival(left_hops - 1, k)
        right_arrival(right_hops - 1, k)
        update = own + from_right[left_hops - 1, :, columns(k)] + from_left[right_hops - 1, :, columns(k)]
        per = n // CHUNKS
        for d in range(per):
            at = k * per + d
            total = pieces[at].astype(jnp.float32) + update[:, d * piece:(d + 1) * piece].astype(jnp.float32)
            out[:, at * piece:(at + 1) * piece] = total.astype(out.dtype)
    for one in started:
        one.wait_send()


def reduce_rows(delta, base, n, snake):
    rows, width = delta.shape[0] // n, delta.shape[1]
    chips = n // 2
    hops = chips // 2
    dma = pltpu.SemaphoreType.DMA
    slots = lambda count: pltpu.VMEM((count, rows, width), delta.dtype)
    return pl.pallas_call(
        functools.partial(reduce_kernel, n, snake),
        out_shape=jax.ShapeDtypeStruct((rows, width), jnp.bfloat16),
        in_specs=[pl.BlockSpec(memory_space=pltpu.VMEM)] * 2,
        out_specs=pl.BlockSpec(memory_space=pltpu.VMEM),
        scratch_shapes=[
            slots(chips), slots(hops), slots(hops), pltpu.VMEM((n, rows, width // n), base.dtype),
            dma((n,)), dma((n,)),
            dma((hops, CHUNKS)), dma((hops, CHUNKS)), dma((hops, CHUNKS)), dma((hops, CHUNKS)),
            dma((chips, CHUNKS)), dma((chips, CHUNKS)),
        ],
        compiler_params=pltpu.CompilerParams(
            collective_id=1, has_side_effects=True, vmem_limit_bytes=52 * 1024 * 1024
        ),
    )(delta, base)


def body(snake, tokens, base_weight, shrink_blocks, expand_blocks, adapter_slot, seg_adapter, seg_lengths):
    my_rows = tokens.shape[0]
    segment_cap = my_rows // seg_adapter.shape[1]
    local_count, rank_size, width = shrink_blocks.shape
    here = lax.axis_index("wide")
    peers = lax.axis_size("wide")
    position = jnp.arange(segment_cap, dtype=jnp.int32)
    my_slot = jnp.take(adapter_slot, seg_adapter.reshape(-1))
    my_row_slot = jnp.where(
        position[None, :] < seg_lengths.reshape(-1, 1), my_slot[:, None], -1
    ).reshape(1, my_rows)
    meta = jnp.broadcast_to(jnp.pad(my_row_slot, ((0, 0), (0, 128 - my_rows))), (8, 128))
    rows, meta_all = gather(tokens, meta, peers, snake)
    row_slot = meta_all[:, 0, :my_rows].reshape(-1)

    column_slot = (
        here * local_count + jnp.arange(local_count * rank_size, dtype=jnp.int32) // rank_size
    )
    selected = row_slot[:, None] == column_slot[None, :]
    shrink = lax.dot_general(
        rows,
        shrink_blocks.reshape(local_count * rank_size, width),
        (((1,), (1,)), ((), ())),
        preferred_element_type=jnp.float32,
    )
    shrink = jnp.where(selected, shrink, jnp.float32(0.0)).astype(jnp.bfloat16)
    delta = jnp.dot(
        shrink,
        expand_blocks.reshape(local_count * rank_size, width),
        preferred_element_type=jnp.float32,
    ).astype(jnp.bfloat16)
    base = jnp.dot(rows, base_weight, preferred_element_type=jnp.float32).astype(jnp.bfloat16)
    return reduce_rows(delta, base, peers, snake)


def solution(mesh):
    placed = (
        P(("groups", "wide"), None),
        P(None, "wide"),
        P("wide", None, None),
        P("wide", None, None),
        P(),
        P(("groups", "wide"), None),
        P(("groups", "wide"), None),
    )
    snake = mesh.shape["groups"] == 2
    return jax.shard_map(
        functools.partial(body, snake), mesh=mesh, in_specs=placed, out_specs=P(("groups", "wide"), None), check_vma=False
    )
```

```python
import functools

import jax
import jax.numpy as jnp
from jax import lax
from jax.experimental import pallas as pl
from jax.experimental.pallas import tpu as pltpu
from jax.sharding import PartitionSpec as P


CHUNKS = 4
MESH = pl.DeviceIdType.MESH


def ring(n, snake):
    me = lax.axis_index("wide")
    chips = n // 2
    core, chip = me % 2, me // 2
    half = chips // 2

    def device(position, on_core):
        at = (position + chips) % chips
        if snake:
            back = at // half
            at = (1 - back) * (2 * at) + back * (2 * (chips - 1 - at) + 1)
        return at * 2 + on_core

    position = chip
    if snake:
        low, high = chip % 2, chip // 2
        position = (1 - low) * high + low * (chips - 1 - high)
    return me, core, position, device


def greet_all(n, me):
    barrier = pltpu.get_barrier_semaphore()
    for step in range(1, n):
        pl.semaphore_signal(
            barrier, inc=1, device_id={"wide": (me + step) % n}, device_id_type=MESH
        )
    pl.semaphore_wait(barrier, n - 1)


def gather_kernel(
    n, snake, tok, meta, out, meta_out, own_sem, meta_send, meta_recv,
    right_send, right_recv, left_send, left_recv, sib_send, sib_recv,
):
    me, core, position, device = ring(n, snake)
    chips = n // 2
    rows, width = tok.shape
    part = width // CHUNKS
    right_hops = chips // 2
    left_hops = chips - 1 - right_hops
    right, left, sibling = device(position + 1, core), device(position - 1, core), device(position, 1 - core)
    greet_all(n, me)

    def place(owner, k):
        return out.at[pl.ds(pl.multiple_of(owner * rows, rows), rows), pl.ds(k * part, part)]

    def copy(src, dst, send, recv, target):
        return pltpu.make_async_remote_copy(
            src_ref=src, dst_ref=dst, send_sem=send, recv_sem=recv,
            device_id={"wide": target}, device_id_type=MESH,
        )

    started = []
    for k in range(CHUNKS):
        src = tok.at[:, pl.ds(k * part, part)]
        started.append(copy(src, place(me, k), right_send.at[0, k], right_recv.at[0, k], right))
        started[-1].start()
        started.append(copy(src, place(me, k), left_send.at[0, k], left_recv.at[0, k], left))
        started[-1].start()
    for step in range(1, n):
        started.append(
            copy(meta, meta_out.at[me], meta_send.at[step], meta_recv.at[step], (me + step) % n)
        )
        started[-1].start()
    for k in range(CHUNKS):
        src = tok.at[:, pl.ds(k * part, part)]
        started.append(copy(src, place(me, k), sib_send.at[0, k], sib_recv.at[0, k], sibling))
        started[-1].start()
    own_rows = pltpu.make_async_copy(tok, out.at[pl.ds(pl.multiple_of(me * rows, rows), rows), :], own_sem.at[0])
    own_meta = pltpu.make_async_copy(meta, meta_out.at[me], own_sem.at[1])
    own_rows.start()
    own_meta.start()

    def by_right(hop, k):
        return hop < right_hops or (hop == right_hops and k < CHUNKS // 2)

    def by_left(hop, k):
        return hop <= left_hops or (hop == right_hops and k >= CHUNKS // 2)

    for hop in range(1, right_hops + 1):
        for k in range(CHUNKS):
            if by_right(hop, k):
                block = place(device(position - hop, core), k)
                copy(block, block, right_send.at[hop - 1, k], right_recv.at[hop - 1, k], right).wait_recv()
                if by_right(hop + 1, k):
                    started.append(copy(block, block, right_send.at[hop, k], right_recv.at[hop, k], right))
                    started[-1].start()
                started.append(copy(block, block, sib_send.at[hop, k], sib_recv.at[hop, k], sibling))
                started[-1].start()
            if by_left(hop, k):
                block = place(device(position + hop, core), k)
                copy(block, block, left_send.at[hop - 1, k], left_recv.at[hop - 1, k], left).wait_recv()
                if by_left(hop + 1, k):
                    started.append(copy(block, block, left_send.at[hop, k], left_recv.at[hop, k], left))
                    started[-1].start()
                at = right_hops + hop if hop <= left_hops else hop
                started.append(copy(block, block, sib_send.at[at, k], sib_recv.at[at, k], sibling))
                started[-1].start()

    for at in range(chips):
        source = position - at if at <= right_hops else position + at - right_hops
        for k in range(CHUNKS):
            block = place(device(source, 1 - core), k)
            copy(block, block, sib_send.at[at, k], sib_recv.at[at, k], sibling).wait_recv()
    for step in range(1, n):
        dst = meta_out.at[(me - step + n) % n]
        copy(meta, dst, meta_send.at[step], meta_recv.at[step], (me + step) % n).wait_recv()
    for one in started:
        one.wait_send()
    own_rows.wait()
    own_meta.wait()


def gather(tokens, meta, n, snake):
    rows, width = tokens.shape
    chips = n // 2
    hops = chips // 2
    dma = pltpu.SemaphoreType.DMA
    return pl.pallas_call(
        functools.partial(gather_kernel, n, snake),
        out_shape=(
            jax.ShapeDtypeStruct((n * rows, width), tokens.dtype),
            jax.ShapeDtypeStruct((n,) + meta.shape, meta.dtype),
        ),
        in_specs=[pl.BlockSpec(memory_space=pl.ANY)] * 2,
        out_specs=(pl.BlockSpec(memory_space=pl.ANY),) * 2,
        scratch_shapes=[
            dma((2,)), dma((n,)), dma((n,)),
            dma((hops, CHUNKS)), dma((hops, CHUNKS)), dma((hops, CHUNKS)), dma((hops, CHUNKS)),
            dma((chips, CHUNKS)), dma((chips, CHUNKS)),
        ],
        compiler_params=pltpu.CompilerParams(collective_id=0, has_side_effects=True),
    )(tokens, meta)


def reduce_kernel(
    n, snake, delta, base, out, sib, from_left, from_right, pieces, base_send, base_recv,
    right_send, right_recv, left_send, left_recv, sib_send, sib_recv,
):
    me, core, position, device = ring(n, snake)
    chips = n // 2
    rows, width = out.shape
    part, piece = width // CHUNKS, width // n
    right_hops = chips // 2
    left_hops = chips - 1 - right_hops
    right, left, sibling = device(position + 1, core), device(position - 1, core), device(position, 1 - core)
    offsets = []
    for hop in range(right_hops):
        offsets.append(right_hops - hop)
        if hop < left_hops:
            offsets.append(hop - left_hops)
    offsets.append(0)
    greet_all(n, me)

    def block(owner):
        return pl.ds(pl.multiple_of(owner * rows, rows), rows)

    def columns(k):
        return pl.ds(k * part, part)

    def copy(src, dst, send, recv, target):
        return pltpu.make_async_remote_copy(
            src_ref=src, dst_ref=dst, send_sem=send, recv_sem=recv,
            device_id={"wide": target}, device_id_type=MESH,
        )

    def sib_copy(j, k):
        return copy(
            delta.at[block(device(position + offsets[j], 1 - core)), columns(k)],
            sib.at[j, :, columns(k)], sib_send.at[j, k], sib_recv.at[j, k], sibling,
        )

    def chip_sum(offset, k):
        j = offsets.index(offset)
        sib_copy(j, k).wait_recv()
        return sib[j, :, columns(k)] + delta[block(device(position + offset, core)), columns(k)]

    def base_copy(step):
        peer = (me + step) % n
        return copy(base.at[block(peer), :], pieces.at[me], base_send.at[step], base_recv.at[step], peer)

    started = []

    def start(one):
        one.start()
        started.append(one)

    def to_right(src, slot, k):
        start(copy(src, from_left.at[slot, :, columns(k)], right_send.at[slot, k], right_recv.at[slot, k], right))

    def to_left(src, slot, k):
        start(copy(src, from_right.at[slot, :, columns(k)], left_send.at[slot, k], left_recv.at[slot, k], left))

    for j in range(chips):
        for k in range(CHUNKS):
            start(sib_copy(j, k))
    for k in range(CHUNKS):
        j = offsets.index(right_hops)
        sib[j, :, columns(k)] = chip_sum(right_hops, k)
        to_right(sib.at[j, :, columns(k)], 0, k)
    for k in range(CHUNKS):
        j = offsets.index(-left_hops)
        sib[j, :, columns(k)] = chip_sum(-left_hops, k)
        to_left(sib.at[j, :, columns(k)], 0, k)
    for step in range(1, n):
        start(base_copy(step))
    pieces[me] = base[block(me), :]

    def right_arrival(slot, k):
        here = from_left.at[slot, :, columns(k)]
        copy(here, here, right_send.at[slot, k], right_recv.at[slot, k], right).wait_recv()

    def left_arrival(slot, k):
        here = from_right.at[slot, :, columns(k)]
        copy(here, here, left_send.at[slot, k], left_recv.at[slot, k], left).wait_recv()

    for hop in range(1, right_hops):
        for k in range(CHUNKS):
            own = chip_sum(right_hops - hop, k)
            right_arrival(hop - 1, k)
            from_left[hop - 1, :, columns(k)] = from_left[hop - 1, :, columns(k)] + own
            to_right(from_left.at[hop - 1, :, columns(k)], hop, k)
            if hop < left_hops:
                own = chip_sum(hop - left_hops, k)
                left_arrival(hop - 1, k)
                from_right[hop - 1, :, columns(k)] = from_right[hop - 1, :, columns(k)] + own
                to_left(from_right.at[hop - 1, :, columns(k)], hop, k)

    for step in range(1, n):
        sender = (me - step + n) % n
        copy(
            base.at[block(sender), :], pieces.at[sender], base_send.at[step], base_recv.at[step], sender
        ).wait_recv()
    for k in range(CHUNKS):
        own = chip_sum(0, k)
        left_arrival(left_hops - 1, k)
        right_arrival(right_hops - 1, k)
        update = own + from_right[left_hops - 1, :, columns(k)] + from_left[right_hops - 1, :, columns(k)]
        per = n // CHUNKS
        for d in range(per):
            at = k * per + d
            total = pieces[at].astype(jnp.float32) + update[:, d * piece:(d + 1) * piece].astype(jnp.float32)
            out[:, at * piece:(at + 1) * piece] = total.astype(out.dtype)
    for one in started:
        one.wait_send()


def reduce_rows(delta, base, n, snake):
    rows, width = delta.shape[0] // n, delta.shape[1]
    chips = n // 2
    hops = chips // 2
    dma = pltpu.SemaphoreType.DMA
    slots = lambda count: pltpu.VMEM((count, rows, width), delta.dtype)
    return pl.pallas_call(
        functools.partial(reduce_kernel, n, snake),
        out_shape=jax.ShapeDtypeStruct((rows, width), jnp.bfloat16),
        in_specs=[pl.BlockSpec(memory_space=pltpu.VMEM)] * 2,
        out_specs=pl.BlockSpec(memory_space=pltpu.VMEM),
        scratch_shapes=[
            slots(chips), slots(hops), slots(hops), pltpu.VMEM((n, rows, width // n), base.dtype),
            dma((n,)), dma((n,)),
            dma((hops, CHUNKS)), dma((hops, CHUNKS)), dma((hops, CHUNKS)), dma((hops, CHUNKS)),
            dma((chips, CHUNKS)), dma((chips, CHUNKS)),
        ],
        compiler_params=pltpu.CompilerParams(
            collective_id=1, has_side_effects=True, vmem_limit_bytes=52 * 1024 * 1024
        ),
    )(delta, base)


def body(snake, tokens, base_weight, shrink_blocks, expand_blocks, adapter_slot, seg_adapter, seg_lengths):
    my_rows = tokens.shape[0]
    segment_cap = my_rows // seg_adapter.shape[1]
    local_count, rank_size, width = shrink_blocks.shape
    here = lax.axis_index("wide")
    peers = lax.axis_size("wide")
    position = jnp.arange(segment_cap, dtype=jnp.int32)
    my_slot = jnp.take(adapter_slot, seg_adapter.reshape(-1))
    my_row_slot = jnp.where(
        position[None, :] < seg_lengths.reshape(-1, 1), my_slot[:, None], -1
    ).reshape(1, my_rows)
    meta = jnp.broadcast_to(jnp.pad(my_row_slot, ((0, 0), (0, 128 - my_rows))), (8, 128))
    rows, meta_all = gather(tokens, meta, peers, snake)
    row_slot = meta_all[:, 0, :my_rows].reshape(-1)

    column_slot = (
        here * local_count + jnp.arange(local_count * rank_size, dtype=jnp.int32) // rank_size
    )
    selected = row_slot[:, None] == column_slot[None, :]
    shrink = lax.dot_general(
        rows,
        shrink_blocks.reshape(local_count * rank_size, width),
        (((1,), (1,)), ((), ())),
        preferred_element_type=jnp.float32,
    )
    shrink = jnp.where(selected, shrink, jnp.float32(0.0)).astype(jnp.bfloat16)
    delta = jnp.dot(
        shrink,
        expand_blocks.reshape(local_count * rank_size, width),
        preferred_element_type=jnp.float32,
    ).astype(jnp.bfloat16)
    base = jnp.dot(rows, base_weight, preferred_element_type=jnp.float32).astype(jnp.bfloat16)
    return reduce_rows(delta, base, peers, snake)


def solution(mesh):
    placed = (
        P(("groups", "wide"), None),
        P(None, "wide"),
        P("wide", None, None),
        P("wide", None, None),
        P(),
        P(("groups", "wide"), None),
        P(("groups", "wide"), None),
    )
    snake = mesh.shape["groups"] == 2
    return jax.shard_map(
        functools.partial(body, snake), mesh=mesh, in_specs=placed, out_specs=P(("groups", "wide"), None), check_vma=False
    )
```

```python
import functools

import jax
import jax.numpy as jnp
from jax import lax
from jax.experimental import pallas as pl
from jax.experimental.pallas import tpu as pltpu
from jax.sharding import PartitionSpec as P


CHUNKS = 4
MESH = pl.DeviceIdType.MESH


def ring(n, snake):
    me = lax.axis_index("wide")
    chips = n // 2
    core, chip = me % 2, me // 2
    half = chips // 2

    def device(position, on_core):
        at = (position + chips) % chips
        if snake:
            back = at // half
            at = (1 - back) * (2 * at) + back * (2 * (chips - 1 - at) + 1)
        return at * 2 + on_core

    position = chip
    if snake:
        low, high = chip % 2, chip // 2
        position = (1 - low) * high + low * (chips - 1 - high)
    return me, core, position, device


def greet_all(n, me):
    barrier = pltpu.get_barrier_semaphore()
    for step in range(1, n):
        pl.semaphore_signal(
            barrier, inc=1, device_id={"wide": (me + step) % n}, device_id_type=MESH
        )
    pl.semaphore_wait(barrier, n - 1)


def gather_kernel(
    n, snake, tok, meta, out, meta_out, own_sem, meta_send, meta_recv,
    right_send, right_recv, left_send, left_recv, sib_send, sib_recv,
):
    me, core, position, device = ring(n, snake)
    chips = n // 2
    rows, width = tok.shape
    part = width // CHUNKS
    right_hops = chips // 2
    right_far = [right_hops if k < CHUNKS // 2 else right_hops - 1 for k in range(CHUNKS)]
    left_far = [chips - 1 - far for far in right_far]
    right, left, sibling = device(position + 1, core), device(position - 1, core), device(position, 1 - core)
    greet_all(n, me)

    def place(owner, k):
        return out.at[pl.ds(pl.multiple_of(owner * rows, rows), rows), pl.ds(k * part, part)]

    def copy(src, dst, send, recv, target):
        return pltpu.make_async_remote_copy(
            src_ref=src, dst_ref=dst, send_sem=send, recv_sem=recv,
            device_id={"wide": target}, device_id_type=MESH,
        )

    started = []
    for k in range(CHUNKS):
        src = tok.at[:, pl.ds(k * part, part)]
        started.append(copy(src, place(me, k), right_send.at[0, k], right_recv.at[0, k], right))
        started[-1].start()
        started.append(copy(src, place(me, k), left_send.at[0, k], left_recv.at[0, k], left))
        started[-1].start()
    for step in range(1, n):
        started.append(
            copy(meta, meta_out.at[me], meta_send.at[step], meta_recv.at[step], (me + step) % n)
        )
        started[-1].start()
    for k in range(CHUNKS):
        src = tok.at[:, pl.ds(k * part, part)]
        started.append(copy(src, place(me, k), sib_send.at[0, k], sib_recv.at[0, k], sibling))
        started[-1].start()
    own_rows = pltpu.make_async_copy(tok, out.at[pl.ds(pl.multiple_of(me * rows, rows), rows), :], own_sem.at[0])
    own_meta = pltpu.make_async_copy(meta, meta_out.at[me], own_sem.at[1])
    own_rows.start()
    own_meta.start()

    for hop in range(1, right_hops + 1):
        for k in range(CHUNKS):
            if hop <= right_far[k]:
                block = place(device(position - hop, core), k)
                copy(block, block, right_send.at[hop - 1, k], right_recv.at[hop - 1, k], right).wait_recv()
                if hop < right_far[k]:
                    started.append(copy(block, block, right_send.at[hop, k], right_recv.at[hop, k], right))
                    started[-1].start()
                started.append(copy(block, block, sib_send.at[hop, k], sib_recv.at[hop, k], sibling))
                started[-1].start()
            if hop <= left_far[k]:
                block = place(device(position + hop, core), k)
                copy(block, block, left_send.at[hop - 1, k], left_recv.at[hop - 1, k], left).wait_recv()
                if hop < left_far[k]:
                    started.append(copy(block, block, left_send.at[hop, k], left_recv.at[hop, k], left))
                    started[-1].start()
                at = right_hops + hop if hop < right_hops else right_hops
                started.append(copy(block, block, sib_send.at[at, k], sib_recv.at[at, k], sibling))
                started[-1].start()

    for at in range(chips):
        source = position - at if at <= right_hops else position + at - right_hops
        for k in range(CHUNKS):
            block = place(device(source, 1 - core), k)
            copy(block, block, sib_send.at[at, k], sib_recv.at[at, k], sibling).wait_recv()
    for step in range(1, n):
        dst = meta_out.at[(me - step + n) % n]
        copy(meta, dst, meta_send.at[step], meta_recv.at[step], (me + step) % n).wait_recv()
    for one in started:
        one.wait_send()
    own_rows.wait()
    own_meta.wait()


def gather(tokens, meta, n, snake):
    rows, width = tokens.shape
    chips = n // 2
    hops = chips // 2
    dma = pltpu.SemaphoreType.DMA
    return pl.pallas_call(
        functools.partial(gather_kernel, n, snake),
        out_shape=(
            jax.ShapeDtypeStruct((n * rows, width), tokens.dtype),
            jax.ShapeDtypeStruct((n,) + meta.shape, meta.dtype),
        ),
        in_specs=[pl.BlockSpec(memory_space=pl.ANY)] * 2,
        out_specs=(pl.BlockSpec(memory_space=pl.ANY),) * 2,
        scratch_shapes=[
            dma((2,)), dma((n,)), dma((n,)),
            dma((hops, CHUNKS)), dma((hops, CHUNKS)), dma((hops, CHUNKS)), dma((hops, CHUNKS)),
            dma((chips, CHUNKS)), dma((chips, CHUNKS)),
        ],
        compiler_params=pltpu.CompilerParams(collective_id=0, has_side_effects=True),
    )(tokens, meta)


def reduce_kernel(
    n, snake, delta, base, out, sib, from_left, from_right, pieces, base_send, base_recv,
    right_send, right_recv, left_send, left_recv, sib_send, sib_recv,
):
    me, core, position, device = ring(n, snake)
    chips = n // 2
    rows, width = out.shape
    part, piece = width // CHUNKS, width // n
    right_hops = chips // 2
    right_far = [right_hops if k < CHUNKS // 2 else right_hops - 1 for k in range(CHUNKS)]
    left_far = [chips - 1 - far for far in right_far]
    right, left, sibling = device(position + 1, core), device(position - 1, core), device(position, 1 - core)
    offsets = [right_hops]
    for far in range(right_hops - 1, 0, -1):
        offsets += [far, -far]
    offsets.append(0)
    greet_all(n, me)

    def block(owner):
        return pl.ds(pl.multiple_of(owner * rows, rows), rows)

    def columns(k):
        return pl.ds(k * part, part)

    def copy(src, dst, send, recv, target):
        return pltpu.make_async_remote_copy(
            src_ref=src, dst_ref=dst, send_sem=send, recv_sem=recv,
            device_id={"wide": target}, device_id_type=MESH,
        )

    def sib_copy(j, k):
        return copy(
            delta.at[block(device(position + offsets[j], 1 - core)), columns(k)],
            sib.at[j, :, columns(k)], sib_send.at[j, k], sib_recv.at[j, k], sibling,
        )

    def chip_sum(offset, k):
        j = offsets.index(right_hops if offset == -right_hops else offset)
        sib_copy(j, k).wait_recv()
        return sib[j, :, columns(k)] + delta[block(device(position + offset, core)), columns(k)]

    def base_copy(step):
        peer = (me + step) % n
        return copy(base.at[block(peer), :], pieces.at[me], base_send.at[step], base_recv.at[step], peer)

    started = []

    def start(one):
        one.start()
        started.append(one)

    def to_right(src, slot, k):
        start(copy(src, from_left.at[slot, :, columns(k)], right_send.at[slot, k], right_recv.at[slot, k], right))

    def to_left(src, slot, k):
        start(copy(src, from_right.at[slot, :, columns(k)], left_send.at[slot, k], left_recv.at[slot, k], left))

    for j in range(chips):
        for k in range(CHUNKS):
            start(sib_copy(j, k))
    for k in range(CHUNKS):
        j = offsets.index(right_far[k])
        sib[j, :, columns(k)] = chip_sum(right_far[k], k)
        to_right(sib.at[j, :, columns(k)], 0, k)
        j = offsets.index(-left_far[k] if left_far[k] < right_hops else right_hops)
        sib[j, :, columns(k)] = chip_sum(-left_far[k], k)
        to_left(sib.at[j, :, columns(k)], 0, k)
    for step in range(1, n):
        start(base_copy(step))
    pieces[me] = base[block(me), :]

    def right_arrival(slot, k):
        here = from_left.at[slot, :, columns(k)]
        copy(here, here, right_send.at[slot, k], right_recv.at[slot, k], right).wait_recv()

    def left_arrival(slot, k):
        here = from_right.at[slot, :, columns(k)]
        copy(here, here, left_send.at[slot, k], left_recv.at[slot, k], left).wait_recv()

    for hop in range(1, right_hops):
        for k in range(CHUNKS):
            if hop < right_far[k]:
                own = chip_sum(right_far[k] - hop, k)
                right_arrival(hop - 1, k)
                from_left[hop - 1, :, columns(k)] = from_left[hop - 1, :, columns(k)] + own
                to_right(from_left.at[hop - 1, :, columns(k)], hop, k)
            if hop < left_far[k]:
                own = chip_sum(hop - left_far[k], k)
                left_arrival(hop - 1, k)
                from_right[hop - 1, :, columns(k)] = from_right[hop - 1, :, columns(k)] + own
                to_left(from_right.at[hop - 1, :, columns(k)], hop, k)

    for step in range(1, n):
        sender = (me - step + n) % n
        copy(
            base.at[block(sender), :], pieces.at[sender], base_send.at[step], base_recv.at[step], sender
        ).wait_recv()
    for k in range(CHUNKS):
        own = chip_sum(0, k)
        left_arrival(left_far[k] - 1, k)
        right_arrival(right_far[k] - 1, k)
        update = own + from_right[left_far[k] - 1, :, columns(k)] + from_left[right_far[k] - 1, :, columns(k)]
        per = n // CHUNKS
        for d in range(per):
            at = k * per + d
            total = pieces[at].astype(jnp.float32) + update[:, d * piece:(d + 1) * piece].astype(jnp.float32)
            out[:, at * piece:(at + 1) * piece] = total.astype(out.dtype)
    for one in started:
        one.wait_send()


def reduce_rows(delta, base, n, snake):
    rows, width = delta.shape[0] // n, delta.shape[1]
    chips = n // 2
    hops = chips // 2
    dma = pltpu.SemaphoreType.DMA
    slots = lambda count: pltpu.VMEM((count, rows, width), delta.dtype)
    return pl.pallas_call(
        functools.partial(reduce_kernel, n, snake),
        out_shape=jax.ShapeDtypeStruct((rows, width), jnp.bfloat16),
        in_specs=[pl.BlockSpec(memory_space=pltpu.VMEM)] * 2,
        out_specs=pl.BlockSpec(memory_space=pltpu.VMEM),
        scratch_shapes=[
            slots(chips), slots(hops), slots(hops), pltpu.VMEM((n, rows, width // n), base.dtype),
            dma((n,)), dma((n,)),
            dma((hops, CHUNKS)), dma((hops, CHUNKS)), dma((hops, CHUNKS)), dma((hops, CHUNKS)),
            dma((chips, CHUNKS)), dma((chips, CHUNKS)),
        ],
        compiler_params=pltpu.CompilerParams(
            collective_id=1, has_side_effects=True, vmem_limit_bytes=52 * 1024 * 1024
        ),
    )(delta, base)


def body(snake, tokens, base_weight, shrink_blocks, expand_blocks, adapter_slot, seg_adapter, seg_lengths):
    my_rows = tokens.shape[0]
    segment_cap = my_rows // seg_adapter.shape[1]
    local_count, rank_size, width = shrink_blocks.shape
    here = lax.axis_index("wide")
    peers = lax.axis_size("wide")
    position = jnp.arange(segment_cap, dtype=jnp.int32)
    my_slot = jnp.take(adapter_slot, seg_adapter.reshape(-1))
    my_row_slot = jnp.where(
        position[None, :] < seg_lengths.reshape(-1, 1), my_slot[:, None], -1
    ).reshape(1, my_rows)
    meta = jnp.broadcast_to(jnp.pad(my_row_slot, ((0, 0), (0, 128 - my_rows))), (8, 128))
    rows, meta_all = gather(tokens, meta, peers, snake)
    row_slot = meta_all[:, 0, :my_rows].reshape(-1)

    column_slot = (
        here * local_count + jnp.arange(local_count * rank_size, dtype=jnp.int32) // rank_size
    )
    selected = row_slot[:, None] == column_slot[None, :]
    shrink = lax.dot_general(
        rows,
        shrink_blocks.reshape(local_count * rank_size, width),
        (((1,), (1,)), ((), ())),
        preferred_element_type=jnp.float32,
    )
    shrink = jnp.where(selected, shrink, jnp.float32(0.0)).astype(jnp.bfloat16)
    delta = jnp.dot(
        shrink,
        expand_blocks.reshape(local_count * rank_size, width),
        preferred_element_type=jnp.float32,
    ).astype(jnp.bfloat16)
    base = jnp.dot(rows, base_weight, preferred_element_type=jnp.float32).astype(jnp.bfloat16)
    return reduce_rows(delta, base, peers, snake)


def solution(mesh):
    placed = (
        P(("groups", "wide"), None),
        P(None, "wide"),
        P("wide", None, None),
        P("wide", None, None),
        P(),
        P(("groups", "wide"), None),
        P(("groups", "wide"), None),
    )
    snake = mesh.shape["groups"] == 2
    return jax.shard_map(
        functools.partial(body, snake), mesh=mesh, in_specs=placed, out_specs=P(("groups", "wide"), None), check_vma=False
    )
```
